512 devices in a mesh: seq: 64 (over z, x), tp: 8 (over y, core).
Axes of the slice: x: 4, y: 4, z: 16, core: 2. Of those that a mesh axis runs over, the one named last changes fastest.
Arguments:
- queries: bfloat16 [32768, 4096], P('seq', 'tp'), may hold values from -6 to 6
- keys: bfloat16 [32768, 4096], P('seq', 'tp'), may hold values from -6 to 6
- values: bfloat16 [32768, 4096], P('seq', 'tp'), may hold values from -6 to 6
- norm_gain: float32 [4096], P('tp'), may hold values from 0.1 to 1.9
- out_weight: bfloat16 [4096, 4096], P('tp', 'seq'), may hold values from -0.25 to 0.25
Outputs:
- mixed: bfloat16 [32768, 4096], P('seq', 'tp')
The draws below stay inside these ranges and needn't reach their ends.
All inputs are finite; a program needn't handle non-finite values.
Results may differ from the reference program's by a relative error of at most 0.017.
Values may be sent and summed in bfloat16 or wider, within the bound.
No kernel may reach another device: no remote copies, remote signals or barrier semaphores. Data moves between devices by JAX's collectives and lax.ppermute only.
A program may use at most 64 MiB of HBM per device.

```python
import jax
import jax.numpy as jnp
from jax import lax

D = 4096
HEADS = 32
HEAD = 128
BLOCK = 512
TOKENS = 32768
N_TP = 8


def spiked(entries, own_key, source, target, blocks, factor):
    def block_of(position):
        return (jnp.arange(entries.shape[position]) // (entries.shape[position] // blocks)).reshape((-1,) + (1,) * (entries.ndim - 1 - position))

    one_side = jax.random.permutation(own_key, blocks)[block_of(target)]
    second = (block_of(target) + blocks // 2) % blocks
    return jnp.where((block_of(source) == one_side) | (block_of(source) == second), factor * entries, entries)


def level_of(rng, shape, pieces, smallest, largest):
    level = 1.0
    for axis_at, blocks in pieces:
        draws = jax.random.uniform(jax.random.fold_in(jax.random.fold_in(rng, 6), axis_at), (blocks,), jnp.float32, smallest / len(pieces), largest / len(pieces))
        level = level * jnp.repeat(jnp.exp(draws), shape[axis_at] // blocks).reshape((-1,) + (1,) * (len(shape) - 1 - axis_at))
    return level


def bell_draw(stream_key, dims, scale, bound, pieces=(), held_as=jnp.bfloat16):
    entries = scale * jax.random.normal(stream_key, dims, jnp.float32)
    if pieces:
        entries = entries * level_of(stream_key, dims, pieces, -0.22, 0.18)
    return jnp.clip(entries, -bound, bound).astype(held_as)


def heavy_noise(rng, shape, deviation, most, split, heavy, dtype=jnp.bfloat16):
    entries = deviation * jax.random.normal(rng, shape, jnp.float32)
    if split:
        entries = entries * level_of(rng, shape, split, -0.22, 0.18)
    return jnp.clip(spiked(entries, jax.random.fold_in(rng, 3), *heavy), -most, most).astype(dtype)


def setup_inputs(seed: int = 0) -> dict:
    key_of = jax.random.split(jax.random.key(seed), 6)
    return {
        "queries": bell_draw(key_of[0], (TOKENS, HEADS * HEAD), 1.0, 6.0, ((0, 64), (1, 8))),
        "keys": bell_draw(key_of[1], (TOKENS, HEADS * HEAD), 1.0, 6.0, ((0, 64), (1, 8))),
        "values": bell_draw(key_of[2], (TOKENS, HEADS * HEAD), 1.0, 6.0, ((0, 64), (1, 8))),
        "norm_gain": jnp.clip(1.0 + 0.18 * jax.random.normal(key_of[3], (HEADS * HEAD,), jnp.float32), 0.1, 1.9),
        "out_weight": heavy_noise(key_of[4], (HEADS * HEAD, D), (HEADS * HEAD) ** -0.5, 0.25, ((0, 8), (1, 64)), (0, 1, 64, 4.0)),
    }


def attend_block(state, block):
    query_blk, key_blk, value_blk, gain = block
    query_f = query_blk.astype(jnp.float32)
    key_f = key_blk.astype(jnp.float32)
    value_f = value_blk.astype(jnp.float32)
    carried = jnp.einsum('thd,hde->the', query_f, state, precision=lax.Precision.HIGHEST)
    scores = jnp.einsum('thd,shd->hts', query_f, key_f, precision=lax.Precision.HIGHEST)
    causal = jnp.arange(BLOCK)[:, None] >= jnp.arange(BLOCK)[None, :]
    weights = jnp.where(causal[None], scores, 0.0).astype(jnp.bfloat16)
    weights = lax.optimization_barrier(weights).astype(jnp.float32)
    local = jnp.einsum('hts,she->the', weights, value_f, precision=lax.Precision.HIGHEST)
    attended = carried + local
    meansq = lax.optimization_barrier(jnp.mean(attended * attended, axis=-1, keepdims=True))
    normed = attended * lax.rsqrt(meansq + 1e-06) * gain
    hidden = normed.reshape(BLOCK, HEADS * HEAD).astype(jnp.bfloat16)
    state = state + jnp.einsum('thd,the->hde', key_f, value_f, precision=lax.Precision.HIGHEST)
    return (state, hidden)

def reference(queries, keys, values, norm_gain, out_weight):
    count = TOKENS // BLOCK
    query_b = queries.reshape(count, BLOCK, HEADS, HEAD)
    key_b = keys.reshape(count, BLOCK, HEADS, HEAD)
    value_b = values.reshape(count, BLOCK, HEADS, HEAD)
    gain = norm_gain.reshape(HEADS, HEAD)

    def step(state, block):
        return attend_block(state, (block[0], block[1], block[2], gain))
    start = jnp.zeros((HEADS, HEAD, HEAD), jnp.float32)
    final, hidden = lax.scan(step, start, (query_b, key_b, value_b))
    hidden = hidden.reshape(TOKENS, HEADS * HEAD)
    group = HEADS * HEAD // N_TP
    total = jnp.zeros((TOKENS, D), jnp.float32)
    for index in range(N_TP):
        partial_sum = jnp.dot(hidden[:, index * group:(index + 1) * group], out_weight[index * group:(index + 1) * group, :], preferred_element_type=jnp.float32)
        partial_sum = lax.optimization_barrier(partial_sum.astype(jnp.bfloat16))
        total = total + partial_sum.astype(jnp.float32)
    return total.astype(jnp.bfloat16)
```

```python
import functools

import jax
import jax.numpy as jnp
from jax import lax
from jax.experimental import pallas as pl
from jax.experimental.pallas import tpu as pltpu
from jax.sharding import Mesh, PartitionSpec as P

HEAD = 128
TILE = 256
NT = (((1,), (1,)), ((), ()))
TN = (((0,), (0,)), ((), ()))


def params():
    return pltpu.CompilerParams(vmem_limit_bytes=40 * 1024 * 1024)


def vmem(count):
    return [pl.BlockSpec(memory_space=pltpu.VMEM)] * count


def block_state_kernel(k_ref, v_ref, s_ref):
    heads = k_ref.shape[1] // HEAD
    for h in range(heads):
        cols = slice(h * HEAD, (h + 1) * HEAD)
        s_ref[cols, :] = lax.dot_general(k_ref[:, cols], v_ref[:, cols], TN, preferred_element_type=jnp.float32)


def block_state(keys, values):
    width = keys.shape[1]
    return pl.pallas_call(
        block_state_kernel,
        out_shape=jax.ShapeDtypeStruct((width, HEAD), jnp.float32),
        in_specs=vmem(2),
        out_specs=pl.BlockSpec(memory_space=pltpu.VMEM),
        compiler_params=params(),
    )(keys, values)


def prefix_kernel(blocks, s_ref, p_ref):
    rows = s_ref.shape[0] // blocks
    total = jnp.zeros((rows, HEAD), jnp.float32)
    for b in range(blocks):
        at = slice(b * rows, (b + 1) * rows)
        p_ref[at, :] = total
        total = total + s_ref[at, :]


def prefix(pieces, blocks):
    return pl.pallas_call(
        functools.partial(prefix_kernel, blocks),
        out_shape=jax.ShapeDtypeStruct(pieces.shape, jnp.float32),
        in_specs=vmem(1),
        out_specs=pl.BlockSpec(memory_space=pltpu.VMEM),
        compiler_params=params(),
    )(pieces)


def attend_kernel(q_ref, k_ref, v_ref, s_ref, g_ref, o_ref):
    rows, width = q_ref.shape
    for h in range(width // HEAD):
        cols = slice(h * HEAD, (h + 1) * HEAD)
        state = s_ref[cols, :]
        high = state.astype(jnp.bfloat16)
        low = (state - high.astype(jnp.float32)).astype(jnp.bfloat16)
        both = jnp.concatenate([high, low], axis=0)
        gain = g_ref[:, cols]
        for first in range(0, rows, TILE):
            own = slice(first, first + TILE)
            seen = first + TILE
            query = q_ref[own, cols]
            carried = jnp.dot(jnp.concatenate([query, query], axis=1), both, preferred_element_type=jnp.float32)
            scores = lax.dot_general(query, k_ref[:seen, cols], NT, preferred_element_type=jnp.float32)
            row = lax.broadcasted_iota(jnp.int32, scores.shape, 0) + first
            col = lax.broadcasted_iota(jnp.int32, scores.shape, 1)
            weights = jnp.where(row >= col, scores, 0.0).astype(jnp.bfloat16)
            local = jnp.dot(weights, v_ref[:seen, cols], preferred_element_type=jnp.float32)
            attended = carried + local
            meansq = jnp.mean(attended * attended, axis=-1, keepdims=True)
            o_ref[own, cols] = (attended * lax.rsqrt(meansq + 1e-06) * gain).astype(jnp.bfloat16)


def attend(queries, keys, values, states, gain):
    return pl.pallas_call(
        attend_kernel,
        out_shape=jax.ShapeDtypeStruct(queries.shape, jnp.bfloat16),
        in_specs=vmem(5),
        out_specs=pl.BlockSpec(memory_space=pltpu.VMEM),
        compiler_params=params(),
    )(queries, keys, values, states, gain)


def shards(queries, keys, values, norm_gain, out_weight):
    blocks = lax.axis_size("z") * lax.axis_size("x")
    near = lax.all_gather(out_weight.T, "x", axis=0, tiled=True)
    near, keys, values = lax.optimization_barrier((near, keys, values))
    weight = lax.all_gather(near, "z", axis=0, tiled=True)
    state = block_state(keys, values)
    pieces = lax.all_to_all(state, ("z", "x"), 0, 0, tiled=True)
    states = lax.all_to_all(prefix(pieces, blocks), ("z", "x"), 0, 0, tiled=True)
    hidden = attend(queries, keys, values, states, norm_gain[None, :])
    partials = lax.dot_general(hidden, weight, NT, preferred_element_type=jnp.float32)
    return lax.psum_scatter(partials.astype(jnp.bfloat16), ("y", "c"), scatter_dimension=1, tiled=True)


def solution(mesh):
    axes = ("z", "x", "y", "c")
    grid = Mesh(mesh.devices.reshape(mesh.devices.shape[0] // 4, 4, 4, 2), axes)
    seq, tp = axes[:2], axes[2:]
    return jax.shard_map(
        shards,
        mesh=grid,
        in_specs=(P(seq, tp), P(seq, tp), P(seq, tp), P(tp), P(tp, seq)),
        out_specs=P(seq, tp),
        check_vma=False,
    )
```

```python
import functools

import jax
import jax.numpy as jnp
from jax import lax
from jax.experimental import pallas as pl
from jax.experimental.pallas import tpu as pltpu
from jax.sharding import Mesh, PartitionSpec as P

HEAD = 128
TILE = 256
GROUP = ("zl", "x")
NT = (((1,), (1,)), ((), ()))
TN = (((0,), (0,)), ((), ()))


def params(mib):
    return pltpu.CompilerParams(vmem_limit_bytes=mib * 1024 * 1024)


def in_vmem():
    return pl.BlockSpec(memory_space=pltpu.VMEM)


def by_head(rows):
    return pl.BlockSpec((rows, HEAD), lambda h: (0, h))


def block_state_kernel(k_ref, v_ref, s_ref):
    s_ref[...] = lax.dot_general(k_ref[...], v_ref[...], TN, preferred_element_type=jnp.float32)


def block_state(keys, values):
    rows, width = keys.shape
    return pl.pallas_call(
        block_state_kernel,
        grid=(width // HEAD,),
        out_shape=jax.ShapeDtypeStruct((width, HEAD), jnp.float32),
        in_specs=[by_head(rows)] * 2,
        out_specs=pl.BlockSpec((HEAD, HEAD), lambda h: (h, 0)),
        compiler_params=params(63),
    )(keys, values)


def total_kernel(s_ref, t_ref):
    rows = t_ref.shape[0]
    total = s_ref[:rows, :]
    for b in range(1, s_ref.shape[0] // rows):
        total = total + s_ref[b * rows:(b + 1) * rows, :]
    t_ref[...] = total


def group_total(pieces, blocks):
    return pl.pallas_call(
        total_kernel,
        out_shape=jax.ShapeDtypeStruct((pieces.shape[0] // blocks, HEAD), jnp.float32),
        in_specs=[in_vmem()],
        out_specs=in_vmem(),
        compiler_params=params(32),
    )(pieces)


def prefix_kernel(group_ref, s_ref, t_ref, p_ref, *, groups):
    rows = t_ref.shape[0] // groups
    total = jnp.zeros((rows, HEAD), jnp.float32)
    for g in range(groups - 1):
        total = total + jnp.where(g < group_ref[0], t_ref[g * rows:(g + 1) * rows, :], 0.0)
    for b in range(s_ref.shape[0] // rows):
        at = slice(b * rows, (b + 1) * rows)
        p_ref[at, :] = total
        total = total + s_ref[at, :]


def prefix(pieces, totals, group, groups):
    return pl.pallas_call(
        functools.partial(prefix_kernel, groups=groups),
        out_shape=jax.ShapeDtypeStruct(pieces.shape, jnp.float32),
        in_specs=[pl.BlockSpec(memory_space=pltpu.SMEM), in_vmem(), in_vmem()],
        out_specs=in_vmem(),
        compiler_params=params(32),
    )(group, pieces, totals)


def attend_kernel(q_ref, k_ref, v_ref, s_ref, g_ref, o_ref):
    rows = q_ref.shape[0]
    state = s_ref[...]
    high = state.astype(jnp.bfloat16)
    low = (state - high.astype(jnp.float32)).astype(jnp.bfloat16)
    both = jnp.concatenate([high, low], axis=0)
    for first in range(0, rows, TILE):
        own = slice(first, first + TILE)
        seen = first + TILE
        query = q_ref[own, :]
        carried = jnp.dot(jnp.concatenate([query, query], axis=1), both, preferred_element_type=jnp.float32)
        scores = lax.dot_general(query, k_ref[:seen, :], NT, preferred_element_type=jnp.float32)
        row = lax.broadcasted_iota(jnp.int32, scores.shape, 0) + first
        col = lax.broadcasted_iota(jnp.int32, scores.shape, 1)
        weights = jnp.where(row >= col, scores, 0.0).astype(jnp.bfloat16)
        local = jnp.dot(weights, v_ref[:seen, :], preferred_element_type=jnp.float32)
        attended = carried + local
        meansq = jnp.mean(attended * attended, axis=-1, keepdims=True)
        o_ref[own, :] = (attended * lax.rsqrt(meansq + 1e-06) * g_ref[...]).astype(jnp.bfloat16)


def attend(queries, keys, values, states, gain):
    rows, width = queries.shape
    return pl.pallas_call(
        attend_kernel,
        grid=(width // HEAD,),
        out_shape=jax.ShapeDtypeStruct(queries.shape, jnp.bfloat16),
        in_specs=[by_head(rows)] * 3 + [pl.BlockSpec((HEAD, HEAD), lambda h: (h, 0)), by_head(1)],
        out_specs=by_head(rows),
        compiler_params=params(63),
    )(queries, keys, values, states, gain)


def project_kernel(order_ref, *refs):
    *hidden_refs, w_ref, o_ref, total = refs
    step = pl.program_id(0)
    for at, h_ref in enumerate(hidden_refs):
        @pl.when(step == at)
        def _():
            part = lax.dot_general(h_ref[...], w_ref[0], NT, preferred_element_type=jnp.float32)
            total[...] = part if at == 0 else total[...] + part

    @pl.when(step == len(hidden_refs) - 1)
    def _():
        o_ref[...] = total[...].astype(o_ref.dtype)


def project(order, hidden, weight):
    groups, columns, depth = weight.shape
    rows = hidden[0].shape[0]
    return pl.pallas_call(
        project_kernel,
        grid_spec=pltpu.PrefetchScalarGridSpec(
            num_scalar_prefetch=1,
            grid=(groups,),
            in_specs=[in_vmem()] * groups
            + [pl.BlockSpec((1, columns, depth), lambda g, order: (order[g], 0, 0))],
            out_specs=pl.BlockSpec((rows, columns), lambda g, order: (0, 0)),
            scratch_shapes=[pltpu.VMEM((rows, columns), jnp.float32)],
        ),
        out_shape=jax.ShapeDtypeStruct((rows, columns), jnp.bfloat16),
        compiler_params=params(47),
    )(order, *hidden, weight)


def shift(array, axis, by):
    size = lax.axis_size(axis)
    return lax.ppermute(array, axis, [(i, (i + by) % size) for i in range(size)])


def to_columns(shard):
    pairs = []
    for z in range(16):
        for t in range(8):
            pairs.append((z * 8 + t, (t * 2 + z % 2) * 8 + z // 2))
    return lax.ppermute(shard, ("zh", "zl", "y", "c"), pairs)


def shards(queries, keys, values, norm_gain, out_weight):
    groups = lax.axis_size("zh")
    blocks = lax.axis_size("zl") * lax.axis_size("x")
    tp = lax.axis_size("y") * lax.axis_size("c")
    near = lax.all_gather(to_columns(out_weight.T), "x", axis=0, tiled=True)
    near, keys, values = lax.optimization_barrier((near, keys, values))
    weight = lax.all_gather(near, ("zh", "zl"), axis=0, tiled=True).reshape(tp, -1, out_weight.shape[0])

    state = block_state(keys, values)
    pieces = lax.all_to_all(state, GROUP, 0, 0, tiled=True)
    totals = lax.all_gather(group_total(pieces, blocks), "zh", axis=0, tiled=True)
    group = lax.axis_index("zh").astype(jnp.int32)[None]
    states = lax.all_to_all(prefix(pieces, totals, group, groups), GROUP, 0, 0, tiled=True)
    hidden = attend(queries, keys, values, states, norm_gain[None, :])

    steps = (0, 1, -1, 2)
    held = [hidden] + [shift(hidden, "y", by) for by in steps[1:]]
    held = held + [shift(h, "c", 1) for h in held]
    row, core = lax.axis_index("y"), lax.axis_index("c")
    place = (row - jnp.array(steps, jnp.int32)) % lax.axis_size("y") * 2
    order = jnp.concatenate([place + core, place + 1 - core]).astype(jnp.int32)
    return project(order, held, weight)


def solution(mesh):
    axes = ("zh", "zl", "x", "y", "c")
    grid = Mesh(mesh.devices.reshape(4, 4, 4, 4, 2), axes)
    seq, tp = axes[:3], axes[3:]
    return jax.shard_map(
        shards,
        mesh=grid,
        in_specs=(P(seq, tp), P(seq, tp), P(seq, tp), P(tp), P(tp, seq)),
        out_specs=P(seq, tp),
        check_vma=False,
    )
```

```python
import functools

import jax
import jax.numpy as jnp
from jax import lax
from jax.experimental import pallas as pl
from jax.experimental.pallas import tpu as pltpu
from jax.sharding import Mesh, PartitionSpec as P

HEAD = 128
TILE = 256
PARTS = 2
AHEAD = 8
GROUP = ("zl", "x")
NT = (((1,), (1,)), ((), ()))
TN = (((0,), (0,)), ((), ()))


def params(mib):
    return pltpu.CompilerParams(vmem_limit_bytes=mib * 1024 * 1024)


def in_vmem():
    return pl.BlockSpec(memory_space=pltpu.VMEM)


def in_hbm():
    return pl.BlockSpec(memory_space=pltpu.HBM)


def fetch(sources, buffers, sems):
    parts = sems.shape[1]
    copies = []
    for part in range(parts):
        for at, (source, buffer) in enumerate(zip(sources, buffers)):
            rows = source.shape[0] // parts
            own = pl.ds(part * rows, rows)
            copies.append(pltpu.make_async_copy(source.at[own], buffer.at[own], sems.at[at, part]))
    for copy in copies:
        copy.start()
    for copy in copies:
        copy.wait()


def block_state_kernel(k_hbm, v_hbm, s_ref, k_ref, v_ref, sems):
    fetch((k_hbm, v_hbm), (k_ref, v_ref), sems)
    for h in range(k_ref.shape[1] // HEAD):
        cols = slice(h * HEAD, (h + 1) * HEAD)
        s_ref[cols, :] = lax.dot_general(k_ref[:, cols], v_ref[:, cols], TN, preferred_element_type=jnp.float32)


def block_state(keys, values):
    return pl.pallas_call(
        block_state_kernel,
        out_shape=jax.ShapeDtypeStruct((keys.shape[1], HEAD), jnp.float32),
        in_specs=[in_hbm()] * 2,
        out_specs=in_vmem(),
        scratch_shapes=[pltpu.VMEM(keys.shape, keys.dtype)] * 2 + [pltpu.SemaphoreType.DMA((2, PARTS))],
        compiler_params=params(32),
    )(keys, values)


def total_kernel(s_ref, t_ref):
    rows = t_ref.shape[0]
    total = s_ref[:rows, :]
    for b in range(1, s_ref.shape[0] // rows):
        total = total + s_ref[b * rows:(b + 1) * rows, :]
    t_ref[...] = total


def group_total(pieces, blocks):
    return pl.pallas_call(
        total_kernel,
        out_shape=jax.ShapeDtypeStruct((pieces.shape[0] // blocks, HEAD), jnp.float32),
        in_specs=[in_vmem()],
        out_specs=in_vmem(),
        compiler_params=params(32),
    )(pieces)


def prefix_kernel(s_ref, *refs):
    *earlier_refs, p_ref = refs
    rows = earlier_refs[0].shape[0]
    total = earlier_refs[0][...]
    for ref in earlier_refs[1:]:
        total = total + ref[...]
    for b in range(s_ref.shape[0] // rows):
        at = slice(b * rows, (b + 1) * rows)
        p_ref[at, :] = total
        total = total + s_ref[at, :]


def prefix(pieces, earlier):
    return pl.pallas_call(
        prefix_kernel,
        out_shape=jax.ShapeDtypeStruct(pieces.shape, jnp.float32),
        in_specs=[in_vmem()] * (1 + len(earlier)),
        out_specs=in_vmem(),
        compiler_params=params(32),
    )(pieces, *earlier)


def attend_kernel(q_hbm, k_hbm, v_hbm, s_ref, g_ref, o_ref, q_ref, k_ref, v_ref, sems):
    fetch((q_hbm, k_hbm, v_hbm), (q_ref, k_ref, v_ref), sems)
    rows, width = o_ref.shape
    row = lax.broadcasted_iota(jnp.int32, (TILE, TILE), 0)
    col = lax.broadcasted_iota(jnp.int32, (TILE, TILE), 1)
    causal = row >= col
    for h in range(width // HEAD):
        cols = slice(h * HEAD, (h + 1) * HEAD)
        state = s_ref[cols, :]
        high = state.astype(jnp.bfloat16)
        low = (state - high.astype(jnp.float32)).astype(jnp.bfloat16)
        for first in range(0, rows, TILE):
            own = slice(first, first + TILE)
            query = q_ref[own, cols]
            scores = lax.dot_general(query, k_ref[:first + TILE, cols], NT, preferred_element_type=jnp.float32)
            left = [query, query, jnp.where(causal, scores[:, first:], 0.0).astype(jnp.bfloat16)]
            right = [high, low, v_ref[own, cols]]
            if first:
                left.append(scores[:, :first].astype(jnp.bfloat16))
                right.append(v_ref[:first, cols])
            left, right = jnp.concatenate(left, axis=1), jnp.concatenate(right, axis=0)
            attended = jnp.dot(left, right, preferred_element_type=jnp.float32)
            meansq = jnp.mean(attended * attended, axis=-1, keepdims=True)
            o_ref[own, cols] = (attended * lax.rsqrt(meansq + 1e-06) * g_ref[:, cols]).astype(jnp.bfloat16)


def attend(queries, keys, values, states, gain):
    return pl.pallas_call(
        attend_kernel,
        out_shape=jax.ShapeDtypeStruct(queries.shape, jnp.bfloat16),
        in_specs=[in_hbm()] * 3 + [in_vmem()] * 2,
        out_specs=in_vmem(),
        scratch_shapes=[pltpu.VMEM(queries.shape, queries.dtype)] * 3 + [pltpu.SemaphoreType.DMA((3, PARTS))],
        compiler_params=params(32),
    )(queries, keys, values, states, gain)


def project_kernel(order_ref, *refs):
    *hidden_hbm, w_hbm, o_ref, h_ref, w_ref, sems = refs
    groups = len(hidden_hbm)

    def copies(at):
        return (
            pltpu.make_async_copy(w_hbm.at[order_ref[at]], w_ref.at[at], sems.at[0, at]),
            pltpu.make_async_copy(hidden_hbm[at], h_ref.at[at], sems.at[1, at]),
        )

    def start(at):
        for copy in copies(at):
            copy.start()

    for at in range(AHEAD):
        start(at)
    total = None
    for at in range(groups):
        for copy in copies(at):
            copy.wait()
        if at + AHEAD < groups:
            start(at + AHEAD)
        product = lax.dot_general(h_ref[at], w_ref[at], NT, preferred_element_type=jnp.float32)
        total = product if total is None else total + product
    o_ref[...] = total.astype(o_ref.dtype)


def project(order, hidden, weight):
    groups = weight.shape[0]
    rows = hidden[0].shape[0]
    return pl.pallas_call(
        project_kernel,
        out_shape=jax.ShapeDtypeStruct((rows, weight.shape[1]), jnp.bfloat16),
        in_specs=[pl.BlockSpec(memory_space=pltpu.SMEM)] + [in_hbm()] * (groups + 1),
        out_specs=in_vmem(),
        scratch_shapes=[
            pltpu.VMEM((groups, *hidden[0].shape), hidden[0].dtype),
            pltpu.VMEM(weight.shape, weight.dtype),
            pltpu.SemaphoreType.DMA((2, groups)),
        ],
        compiler_params=params(62),
    )(order, *hidden, weight)


def shift(array, axis, by):
    size = lax.axis_size(axis)
    return lax.ppermute(array, axis, [(i, (i + by) % size) for i in range(size)])


def from_earlier(array, axis, by):
    size = lax.axis_size(axis)
    return lax.ppermute(array, axis, [(i, i + by) for i in range(size - by)])


def spread(array, axis):
    return lax.all_to_all(jnp.concatenate([array] * lax.axis_size(axis), axis=0), axis, 0, 0, tiled=True)


def turn(place):
    row, core = place // 2, place % 2
    return row * (1 - 2 * core) + 4 * core * (row == 0)


def to_columns(shard):
    pairs = []
    for z in range(16):
        for t in range(8):
            pairs.append((z * 8 + t, (z + 2 * turn(t)) % 16 * 8 + z // 2))
    return lax.ppermute(shard, ("zh", "zl", "y", "c"), pairs)


def shards(queries, keys, values, norm_gain, out_weight):
    blocks = lax.axis_size("zl") * lax.axis_size("x")
    tp = lax.axis_size("y") * lax.axis_size("c")
    shard, state = lax.optimization_barrier((to_columns(out_weight.T), block_state(keys, values)))
    near = spread(shard, "x")
    pieces = lax.all_to_all(state, GROUP, 0, 0, tiled=True)
    weight = lax.all_gather(near, ("zh", "zl"), axis=0, tiled=True)
    weight = weight.reshape(tp, -1, out_weight.shape[0])

    total = group_total(pieces, blocks)
    earlier = [from_earlier(total, "zh", by) for by in range(1, lax.axis_size("zh"))]
    states = lax.all_to_all(prefix(pieces, earlier), GROUP, 0, 0, tiled=True)
    hidden = attend(queries, keys, values, states, norm_gain[None, :])

    steps = (0, 1, -1, 2)
    held = [hidden] + [shift(hidden, "y", by) for by in steps[1:]]
    held = held + [shift(h, "c", 1) for h in held]
    row, core = lax.axis_index("y"), lax.axis_index("c")
    place = (row - jnp.array(steps, jnp.int32)) % lax.axis_size("y") * 2
    place = jnp.concatenate([place + core, place + 1 - core])
    order = (row * 2 + core + turn(place)) % tp
    return project(order.astype(jnp.int32), held, weight)


def solution(mesh):
    axes = ("zh", "zl", "x", "y", "c")
    grid = Mesh(mesh.devices.reshape(4, 4, 4, 4, 2), axes)
    seq, tp = axes[:3], axes[3:]
    return jax.shard_map(
        shards,
        mesh=grid,
        in_specs=(P(seq, tp), P(seq, tp), P(seq, tp), P(tp), P(tp, seq)),
        out_specs=P(seq, tp),
        check_vma=False,
    )
```

```python
import functools

import jax
import jax.numpy as jnp
from jax import lax
from jax.experimental import pallas as pl
from jax.experimental.pallas import tpu as pltpu
from jax.sharding import Mesh, PartitionSpec as P

HEAD = 128
TILE = 256
PARTS = 2
AHEAD = 8
GROUP = ("zl", "x")
NT = (((1,), (1,)), ((), ()))
TN = (((0,), (0,)), ((), ()))


def params(mib):
    return pltpu.CompilerParams(vmem_limit_bytes=mib * 1024 * 1024)


def in_vmem():
    return pl.BlockSpec(memory_space=pltpu.VMEM)


def in_hbm():
    return pl.BlockSpec(memory_space=pltpu.HBM)


def fetch(sources, buffers, sems):
    parts = sems.shape[1]
    copies = []
    for part in range(parts):
        for at, (source, buffer) in enumerate(zip(sources, buffers)):
            rows = source.shape[0] // parts
            own = pl.ds(part * rows, rows)
            copies.append(pltpu.make_async_copy(source.at[own], buffer.at[own], sems.at[at, part]))
    for copy in copies:
        copy.start()
    for copy in copies:
        copy.wait()


def block_state_kernel(k_hbm, v_hbm, s_ref, k_ref, v_ref, sems):
    fetch((k_hbm, v_hbm), (k_ref, v_ref), sems)
    for h in range(k_ref.shape[1] // HEAD):
        cols = slice(h * HEAD, (h + 1) * HEAD)
        s_ref[cols, :] = lax.dot_general(k_ref[:, cols], v_ref[:, cols], TN, preferred_element_type=jnp.float32)


def block_state(keys, values):
    return pl.pallas_call(
        block_state_kernel,
        out_shape=jax.ShapeDtypeStruct((keys.shape[1], HEAD), jnp.float32),
        in_specs=[in_hbm()] * 2,
        out_specs=in_vmem(),
        scratch_shapes=[pltpu.VMEM(keys.shape, keys.dtype)] * 2 + [pltpu.SemaphoreType.DMA((2, PARTS))],
        compiler_params=params(32),
    )(keys, values)


def total_kernel(s_ref, t_ref):
    rows = t_ref.shape[0]
    total = s_ref[:rows, :]
    for b in range(1, s_ref.shape[0] // rows):
        total = total + s_ref[b * rows:(b + 1) * rows, :]
    t_ref[...] = total


def group_total(pieces, blocks):
    return pl.pallas_call(
        total_kernel,
        out_shape=jax.ShapeDtypeStruct((pieces.shape[0] // blocks, HEAD), jnp.float32),
        in_specs=[in_vmem()],
        out_specs=in_vmem(),
        compiler_params=params(32),
    )(pieces)


def prefix_kernel(s_ref, *refs):
    *earlier_refs, p_ref = refs
    rows = earlier_refs[0].shape[0]
    total = earlier_refs[0][...]
    for ref in earlier_refs[1:]:
        total = total + ref[...]
    for b in range(s_ref.shape[0] // rows):
        at = slice(b * rows, (b + 1) * rows)
        p_ref[at, :] = total
        total = total + s_ref[at, :]


def prefix(pieces, earlier):
    return pl.pallas_call(
        prefix_kernel,
        out_shape=jax.ShapeDtypeStruct(pieces.shape, jnp.float32),
        in_specs=[in_vmem()] * (1 + len(earlier)),
        out_specs=in_vmem(),
        compiler_params=params(32),
    )(pieces, *earlier)


def attend_kernel(q_hbm, k_hbm, v_hbm, s_ref, g_ref, o_ref, q_ref, k_ref, v_ref, sems):
    fetch((q_hbm, k_hbm, v_hbm), (q_ref, k_ref, v_ref), sems)
    rows, width = o_ref.shape
    row = lax.broadcasted_iota(jnp.int32, (TILE, TILE), 0)
    col = lax.broadcasted_iota(jnp.int32, (TILE, TILE), 1)
    causal = row >= col
    for h in range(width // HEAD):
        cols = slice(h * HEAD, (h + 1) * HEAD)
        state = s_ref[cols, :]
        high = state.astype(jnp.bfloat16)
        low = (state - high.astype(jnp.float32)).astype(jnp.bfloat16)
        for first in range(0, rows, TILE):
            own = slice(first, first + TILE)
            query = q_ref[own, cols]
            scores = lax.dot_general(query, k_ref[:first + TILE, cols], NT, preferred_element_type=jnp.float32)
            left = [query, query, jnp.where(causal, scores[:, first:], 0.0).astype(jnp.bfloat16)]
            right = [high, low, v_ref[own, cols]]
            if first:
                left.append(scores[:, :first].astype(jnp.bfloat16))
                right.append(v_ref[:first, cols])
            left, right = jnp.concatenate(left, axis=1), jnp.concatenate(right, axis=0)
            attended = jnp.dot(left, right, preferred_element_type=jnp.float32)
            meansq = jnp.mean(attended * attended, axis=-1, keepdims=True)
            o_ref[own, cols] = (attended * lax.rsqrt(meansq + 1e-06) * g_ref[:, cols]).astype(jnp.bfloat16)


def attend(queries, keys, values, states, gain):
    return pl.pallas_call(
        attend_kernel,
        out_shape=jax.ShapeDtypeStruct(queries.shape, jnp.bfloat16),
        in_specs=[in_hbm()] * 3 + [in_vmem()] * 2,
        out_specs=in_vmem(),
        scratch_shapes=[pltpu.VMEM(queries.shape, queries.dtype)] * 3 + [pltpu.SemaphoreType.DMA((3, PARTS))],
        compiler_params=params(32),
    )(queries, keys, values, states, gain)


def project_kernel(order_ref, *refs):
    *hidden_hbm, w_hbm, o_ref, h_ref, w_ref, sems = refs
    groups = len(hidden_hbm)

    def copies(at):
        return (
            pltpu.make_async_copy(w_hbm.at[order_ref[at]], w_ref.at[at], sems.at[0, at]),
            pltpu.make_async_copy(hidden_hbm[at], h_ref.at[at], sems.at[1, at]),
        )

    def start(at):
        for copy in copies(at):
            copy.start()

    for at in range(AHEAD):
        start(at)
    total = None
    for at in range(groups):
        for copy in copies(at):
            copy.wait()
        if at + AHEAD < groups:
            start(at + AHEAD)
        product = lax.dot_general(h_ref[at], w_ref[at], NT, preferred_element_type=jnp.float32)
        total = product if total is None else total + product
    o_ref[...] = total.astype(o_ref.dtype)


def project(order, hidden, weight):
    groups = weight.shape[0]
    rows = hidden[0].shape[0]
    return pl.pallas_call(
        project_kernel,
        out_shape=jax.ShapeDtypeStruct((rows, weight.shape[1]), jnp.bfloat16),
        in_specs=[pl.BlockSpec(memory_space=pltpu.SMEM)] + [pl.BlockSpec(memory_space=pl.ANY)] * groups + [in_hbm()],
        out_specs=in_vmem(),
        scratch_shapes=[
            pltpu.VMEM((groups, *hidden[0].shape), hidden[0].dtype),
            pltpu.VMEM(weight.shape, weight.dtype),
            pltpu.SemaphoreType.DMA((2, groups)),
        ],
        compiler_params=params(51),
    )(order, *hidden, weight)


def shift(array, axis, by):
    size = lax.axis_size(axis)
    return lax.ppermute(array, axis, [(i, (i + by) % size) for i in range(size)])


def from_earlier(array, axis, by):
    size = lax.axis_size(axis)
    return lax.ppermute(array, axis, [(i, i + by) for i in range(size - by)])


def spread(array, axis):
    copies = jnp.broadcast_to(array, (lax.axis_size(axis), *array.shape))
    return lax.all_to_all(copies, axis, 0, 0, tiled=True).reshape(-1, *array.shape[1:])


TURN = ((4, 3), (-3, 2), (0, -1), (-2, 1))


def to_columns(shard):
    pairs = []
    for z in range(16):
        for t in range(8):
            goal = z // 2
            far = TURN[(t // 2 - goal // 2) % 4][t % 2]
            pairs.append((z * 8 + t, (z + 2 * far) % 16 * 8 + goal))
    return lax.ppermute(shard, ("zh", "zl", "y", "c"), pairs)


def shards(queries, keys, values, norm_gain, out_weight):
    blocks = lax.axis_size("zl") * lax.axis_size("x")
    tp = lax.axis_size("y") * lax.axis_size("c")
    shard, state = lax.optimization_barrier((to_columns(out_weight.T), block_state(keys, values)))
    near = spread(shard, "x")
    pieces = lax.all_to_all(state, GROUP, 0, 0, tiled=True)
    weight = lax.all_gather(near, ("zh", "zl"), axis=0, tiled=True)
    weight = weight.reshape(tp, -1, out_weight.shape[0])

    total = group_total(pieces, blocks)
    earlier = []
    for group in range(lax.axis_size("zh") - 1):
        passed = total + earlier[-1] if earlier else total
        earlier.append(lax.ppermute(passed, "zh", [(group, group + 1)]))
    states = lax.all_to_all(prefix(pieces, earlier), GROUP, 0, 0, tiled=True)
    hidden = attend(queries, keys, values, states, norm_gain[None, :])

    steps = (0, 1, -1, 2)
    held = [hidden] + [shift(hidden, "y", by) for by in steps[1:]]
    held = held + [shift(h, "c", 1) for h in held]
    row, core = lax.axis_index("y"), lax.axis_index("c")
    far = jnp.array([TURN[-by % 4] for by in steps], jnp.int32)
    far = jnp.where(core == 0, far, far[:, ::-1]).T.reshape(-1)
    order = (row * 2 + core + far) % tp
    return project(order.astype(jnp.int32), held, weight)


def solution(mesh):
    axes = ("zh", "zl", "x", "y", "c")
    grid = Mesh(mesh.devices.reshape(4, 4, 4, 4, 2), axes)
    seq, tp = axes[:3], axes[3:]
    return jax.shard_map(
        shards,
        mesh=grid,
        in_specs=(P(seq, tp), P(seq, tp), P(seq, tp), P(tp), P(tp, seq)),
        out_specs=P(seq, tp),
        check_vma=False,
    )
```

```python
import functools

import jax
import jax.numpy as jnp
from jax import lax
from jax.experimental import pallas as pl
from jax.experimental.pallas import tpu as pltpu
from jax.sharding import Mesh, PartitionSpec as P

HEAD = 128
TILE = 256
PARTS = 2
AHEAD = 8
GROUP = ("zl", "x")
NT = (((1,), (1,)), ((), ()))
TN = (((0,), (0,)), ((), ()))


def params(mib):
    return pltpu.CompilerParams(vmem_limit_bytes=mib * 1024 * 1024)


def in_vmem():
    return pl.BlockSpec(memory_space=pltpu.VMEM)


def in_hbm():
    return pl.BlockSpec(memory_space=pltpu.HBM)


def fetch(sources, buffers, sems):
    parts = sems.shape[1]
    copies = []
    for part in range(parts):
        for at, (source, buffer) in enumerate(zip(sources, buffers)):
            rows = source.shape[0] // parts
            own = pl.ds(part * rows, rows)
            copies.append(pltpu.make_async_copy(source.at[own], buffer.at[own], sems.at[at, part]))
    for copy in copies:
        copy.start()
    for copy in copies:
        copy.wait()


def block_state_kernel(k_hbm, v_hbm, s_ref, k_ref, v_ref, sems):
    fetch((k_hbm, v_hbm), (k_ref, v_ref), sems)
    for h in range(k_ref.shape[1] // HEAD):
        cols = slice(h * HEAD, (h + 1) * HEAD)
        s_ref[cols, :] = lax.dot_general(k_ref[:, cols], v_ref[:, cols], TN, preferred_element_type=jnp.float32)


def block_state(keys, values):
    return pl.pallas_call(
        block_state_kernel,
        out_shape=jax.ShapeDtypeStruct((keys.shape[1], HEAD), jnp.float32),
        in_specs=[in_hbm()] * 2,
        out_specs=in_vmem(),
        scratch_shapes=[pltpu.VMEM(keys.shape, keys.dtype)] * 2 + [pltpu.SemaphoreType.DMA((2, PARTS))],
        compiler_params=params(32),
    )(keys, values)


def total_kernel(s_ref, t_ref):
    rows = t_ref.shape[0]
    total = s_ref[:rows, :]
    for b in range(1, s_ref.shape[0] // rows):
        total = total + s_ref[b * rows:(b + 1) * rows, :]
    t_ref[...] = total


def group_total(pieces, blocks):
    return pl.pallas_call(
        total_kernel,
        out_shape=jax.ShapeDtypeStruct((pieces.shape[0] // blocks, HEAD), jnp.float32),
        in_specs=[in_vmem()],
        out_specs=in_vmem(),
        compiler_params=params(32),
    )(pieces)


def prefix_kernel(s_ref, *refs):
    *earlier_refs, p_ref = refs
    rows = earlier_refs[0].shape[0]
    total = earlier_refs[0][...]
    for ref in earlier_refs[1:]:
        total = total + ref[...]
    for b in range(s_ref.shape[0] // rows):
        at = slice(b * rows, (b + 1) * rows)
        p_ref[at, :] = total
        total = total + s_ref[at, :]


def prefix(pieces, earlier):
    return pl.pallas_call(
        prefix_kernel,
        out_shape=jax.ShapeDtypeStruct(pieces.shape, jnp.float32),
        in_specs=[in_vmem()] * (1 + len(earlier)),
        out_specs=in_vmem(),
        compiler_params=params(32),
    )(pieces, *earlier)


def attend_kernel(q_hbm, k_hbm, v_hbm, s_ref, g_ref, o_ref, q_ref, k_ref, v_ref, sems):
    fetch((q_hbm, k_hbm, v_hbm), (q_ref, k_ref, v_ref), sems)
    rows, width = o_ref.shape
    row = lax.broadcasted_iota(jnp.int32, (TILE, TILE), 0)
    col = lax.broadcasted_iota(jnp.int32, (TILE, TILE), 1)
    causal = row >= col
    for h in range(width // HEAD):
        cols = slice(h * HEAD, (h + 1) * HEAD)
        state = s_ref[cols, :]
        high = state.astype(jnp.bfloat16)
        low = (state - high.astype(jnp.float32)).astype(jnp.bfloat16)
        for first in range(0, rows, TILE):
            own = slice(first, first + TILE)
            query = q_ref[own, cols]
            scores = lax.dot_general(query, k_ref[:first + TILE, cols], NT, preferred_element_type=jnp.float32)
            left = [query, query, jnp.where(causal, scores[:, first:], 0.0).astype(jnp.bfloat16)]
            right = [high, low, v_ref[own, cols]]
            if first:
                left.append(scores[:, :first].astype(jnp.bfloat16))
                right.append(v_ref[:first, cols])
            left, right = jnp.concatenate(left, axis=1), jnp.concatenate(right, axis=0)
            attended = jnp.dot(left, right, preferred_element_type=jnp.float32)
            meansq = jnp.mean(attended * attended, axis=-1, keepdims=True)
            o_ref[own, cols] = (attended * lax.rsqrt(meansq + 1e-06) * g_ref[:, cols]).astype(jnp.bfloat16)


def attend(queries, keys, values, states, gain):
    return pl.pallas_call(
        attend_kernel,
        out_shape=jax.ShapeDtypeStruct(queries.shape, jnp.bfloat16),
        in_specs=[in_hbm()] * 3 + [in_vmem()] * 2,
        out_specs=in_vmem(),
        scratch_shapes=[pltpu.VMEM(queries.shape, queries.dtype)] * 3 + [pltpu.SemaphoreType.DMA((3, PARTS))],
        compiler_params=params(32),
    )(queries, keys, values, states, gain)


def project_kernel(order_ref, *refs):
    *hidden_hbm, w_hbm, o_ref, h_ref, w_ref, sems = refs
    groups = len(hidden_hbm)

    def copies(at):
        return (
            pltpu.make_async_copy(w_hbm.at[order_ref[at]], w_ref.at[at], sems.at[0, at]),
            pltpu.make_async_copy(hidden_hbm[at], h_ref.at[at], sems.at[1, at]),
        )

    def start(at):
        for copy in copies(at):
            copy.start()

    for at in range(AHEAD):
        start(at)
    total = None
    for at in range(groups):
        for copy in copies(at):
            copy.wait()
        if at + AHEAD < groups:
            start(at + AHEAD)
        product = lax.dot_general(h_ref[at], w_ref[at], NT, preferred_element_type=jnp.float32)
        total = product if total is None else total + product
    o_ref[...] = total.astype(o_ref.dtype)


def project(order, hidden, weight):
    groups = weight.shape[0]
    rows = hidden[0].shape[0]
    return pl.pallas_call(
        project_kernel,
        out_shape=jax.ShapeDtypeStruct((rows, weight.shape[1]), jnp.bfloat16),
        in_specs=[pl.BlockSpec(memory_space=pltpu.SMEM)] + [pl.BlockSpec(memory_space=pl.ANY)] * groups + [in_hbm()],
        out_specs=in_vmem(),
        scratch_shapes=[
            pltpu.VMEM((groups, *hidden[0].shape), hidden[0].dtype),
            pltpu.VMEM(weight.shape, weight.dtype),
            pltpu.SemaphoreType.DMA((2, groups)),
        ],
        compiler_params=params(51),
    )(order, *hidden, weight)


def shift(array, axis, by):
    size = lax.axis_size(axis)
    return lax.ppermute(array, axis, [(i, (i + by) % size) for i in range(size)])


def from_earlier(array, axis, by):
    size = lax.axis_size(axis)
    return lax.ppermute(array, axis, [(i, i + by) for i in range(size - by)])


def spread(array, axis):
    copies = jnp.broadcast_to(array, (lax.axis_size(axis), *array.shape))
    return lax.all_to_all(copies, axis, 0, 0, tiled=True).reshape(-1, *array.shape[1:])


TURN = ((4, -3), (3, -2), (0, 1), (2, -1))


def to_columns(shard):
    pairs = []
    for z in range(16):
        for t in range(8):
            goal = z // 2
            far = TURN[(t // 2 - goal // 2) % 4][t % 2]
            pairs.append((z * 8 + t, (z + 2 * far) % 16 * 8 + goal))
    return lax.ppermute(shard, ("zh", "zl", "y", "c"), pairs)


def shards(queries, keys, values, norm_gain, out_weight):
    blocks = lax.axis_size("zl") * lax.axis_size("x")
    tp = lax.axis_size("y") * lax.axis_size("c")
    shard, state = lax.optimization_barrier((to_columns(out_weight.T), block_state(keys, values)))
    near = spread(shard, "x")
    pieces = lax.all_to_all(state, GROUP, 0, 0, tiled=True)
    weight = lax.all_gather(near, ("zh", "zl"), axis=0, tiled=True)
    weight = weight.reshape(tp, -1, out_weight.shape[0])

    total = group_total(pieces, blocks)
    earlier = []
    for group in range(lax.axis_size("zh") - 1):
        passed = total + earlier[-1] if earlier else total
        earlier.append(lax.ppermute(passed, "zh", [(group, group + 1)]))
    states = lax.all_to_all(prefix(pieces, earlier), GROUP, 0, 0, tiled=True)
    hidden = attend(queries, keys, values, states, norm_gain[None, :])

    steps = (0, 1, -1, 2)
    held = [hidden] + [shift(hidden, "y", by) for by in steps[1:]]
    held = held + [shift(h, "c", 1) for h in held]
    row, core = lax.axis_index("y"), lax.axis_index("c")
    far = jnp.array([TURN[-by % 4] for by in steps], jnp.int32)
    far = jnp.where(core == 0, far, far[:, ::-1]).T.reshape(-1)
    order = (row * 2 + core + far) % tp
    return project(order.astype(jnp.int32), held, weight)


def solution(mesh):
    axes = ("zh", "zl", "x", "y", "c")
    grid = Mesh(mesh.devices.reshape(4, 4, 4, 4, 2), axes)
    seq, tp = axes[:3], axes[3:]
    return jax.shard_map(
        shards,
        mesh=grid,
        in_specs=(P(seq, tp), P(seq, tp), P(seq, tp), P(tp), P(tp, seq)),
        out_specs=P(seq, tp),
        check_vma=False,
    )
```

```python
import functools

import jax
import jax.numpy as jnp
from jax import lax
from jax.experimental import pallas as pl
from jax.experimental.pallas import tpu as pltpu
from jax.sharding import Mesh, PartitionSpec as P

HEAD = 128
TILE = 256
PARTS = 2
AHEAD = 8
GROUP = ("x", "zl")
NT = (((1,), (1,)), ((), ()))
TN = (((0,), (0,)), ((), ()))


def params(mib):
    return pltpu.CompilerParams(vmem_limit_bytes=mib * 1024 * 1024)


def in_vmem():
    return pl.BlockSpec(memory_space=pltpu.VMEM)


def in_hbm():
    return pl.BlockSpec(memory_space=pltpu.HBM)


def fetch(sources, buffers, sems):
    parts = sems.shape[1]
    copies = []
    for part in range(parts):
        for at, (source, buffer) in enumerate(zip(sources, buffers)):
            rows = source.shape[0] // parts
            own = pl.ds(part * rows, rows)
            copies.append(pltpu.make_async_copy(source.at[own], buffer.at[own], sems.at[at, part]))
    for copy in copies:
        copy.start()
    for copy in copies:
        copy.wait()


def block_state_kernel(k_hbm, v_hbm, s_ref, k_ref, v_ref, sems):
    fetch((k_hbm, v_hbm), (k_ref, v_ref), sems)
    for h in range(k_ref.shape[1] // HEAD):
        cols = slice(h * HEAD, (h + 1) * HEAD)
        s_ref[cols, :] = lax.dot_general(k_ref[:, cols], v_ref[:, cols], TN, preferred_element_type=jnp.float32)


def block_state(keys, values):
    return pl.pallas_call(
        block_state_kernel,
        out_shape=jax.ShapeDtypeStruct((keys.shape[1], HEAD), jnp.float32),
        in_specs=[in_hbm()] * 2,
        out_specs=in_vmem(),
        scratch_shapes=[pltpu.VMEM(keys.shape, keys.dtype)] * 2 + [pltpu.SemaphoreType.DMA((2, PARTS))],
        compiler_params=params(32),
    )(keys, values)


def total_kernel(s_ref, t_ref):
    rows = t_ref.shape[0]
    total = s_ref[:rows, :]
    for b in range(1, s_ref.shape[0] // rows):
        total = total + s_ref[b * rows:(b + 1) * rows, :]
    t_ref[...] = total


def group_total(pieces, blocks):
    return pl.pallas_call(
        total_kernel,
        out_shape=jax.ShapeDtypeStruct((pieces.shape[0] // blocks, HEAD), jnp.float32),
        in_specs=[in_vmem()],
        out_specs=in_vmem(),
        compiler_params=params(32),
    )(pieces)


def prefix_kernel(s_ref, *refs):
    *earlier_refs, p_ref = refs
    rows = earlier_refs[0].shape[0]
    total = earlier_refs[0][...]
    for ref in earlier_refs[1:]:
        total = total + ref[...]
    for b in range(s_ref.shape[0] // rows):
        place = b % 4 * 4 + b // 4
        at = slice(place * rows, (place + 1) * rows)
        p_ref[at, :] = total
        total = total + s_ref[at, :]


def prefix(pieces, earlier):
    return pl.pallas_call(
        prefix_kernel,
        out_shape=jax.ShapeDtypeStruct(pieces.shape, jnp.float32),
        in_specs=[in_vmem()] * (1 + len(earlier)),
        out_specs=in_vmem(),
        compiler_params=params(32),
    )(pieces, *earlier)


def attend_kernel(q_hbm, k_hbm, v_hbm, s_ref, g_ref, o_ref, q_ref, k_ref, v_ref, sems):
    fetch((q_hbm, k_hbm, v_hbm), (q_ref, k_ref, v_ref), sems)
    rows, width = o_ref.shape
    row = lax.broadcasted_iota(jnp.int32, (TILE, TILE), 0)
    col = lax.broadcasted_iota(jnp.int32, (TILE, TILE), 1)
    causal = row >= col
    for h in range(width // HEAD):
        cols = slice(h * HEAD, (h + 1) * HEAD)
        state = s_ref[cols, :]
        high = state.astype(jnp.bfloat16)
        low = (state - high.astype(jnp.float32)).astype(jnp.bfloat16)
        for first in range(0, rows, TILE):
            own = slice(first, first + TILE)
            query = q_ref[own, cols]
            scores = lax.dot_general(query, k_ref[:first + TILE, cols], NT, preferred_element_type=jnp.float32)
            left = [query, query, jnp.where(causal, scores[:, first:], 0.0).astype(jnp.bfloat16)]
            right = [high, low, v_ref[own, cols]]
            if first:
                left.append(scores[:, :first].astype(jnp.bfloat16))
                right.append(v_ref[:first, cols])
            left, right = jnp.concatenate(left, axis=1), jnp.concatenate(right, axis=0)
            attended = jnp.dot(left, right, preferred_element_type=jnp.float32)
            meansq = jnp.mean(attended * attended, axis=-1, keepdims=True)
            o_ref[own, cols] = (attended * lax.rsqrt(meansq + 1e-06) * g_ref[:, cols]).astype(jnp.bfloat16)


def attend(queries, keys, values, states, gain):
    return pl.pallas_call(
        attend_kernel,
        out_shape=jax.ShapeDtypeStruct(queries.shape, jnp.bfloat16),
        in_specs=[in_hbm()] * 3 + [in_vmem()] * 2,
        out_specs=in_vmem(),
        scratch_shapes=[pltpu.VMEM(queries.shape, queries.dtype)] * 3 + [pltpu.SemaphoreType.DMA((3, PARTS))],
        compiler_params=params(32),
    )(queries, keys, values, states, gain)


def project_kernel(order_ref, *refs):
    *hidden_hbm, w_hbm, o_ref, h_ref, w_ref, sems = refs
    groups = len(hidden_hbm)

    def copies(at):
        return (
            pltpu.make_async_copy(w_hbm.at[order_ref[at]], w_ref.at[at], sems.at[0, at]),
            pltpu.make_async_copy(hidden_hbm[at], h_ref.at[at], sems.at[1, at]),
        )

    def start(at):
        for copy in copies(at):
            copy.start()

    for at in range(AHEAD):
        start(at)
    total = None
    for at in range(groups):
        for copy in copies(at):
            copy.wait()
        if at + AHEAD < groups:
            start(at + AHEAD)
        product = lax.dot_general(h_ref[at], w_ref[at], NT, preferred_element_type=jnp.float32)
        total = product if total is None else total + product
    o_ref[...] = total.astype(o_ref.dtype)


def project(order, hidden, weight):
    groups = weight.shape[0]
    rows = hidden[0].shape[0]
    return pl.pallas_call(
        project_kernel,
        out_shape=jax.ShapeDtypeStruct((rows, weight.shape[1]), jnp.bfloat16),
        in_specs=[pl.BlockSpec(memory_space=pltpu.SMEM)] + [pl.BlockSpec(memory_space=pl.ANY)] * groups + [in_hbm()],
        out_specs=in_vmem(),
        scratch_shapes=[
            pltpu.VMEM((groups, *hidden[0].shape), hidden[0].dtype),
            pltpu.VMEM(weight.shape, weight.dtype),
            pltpu.SemaphoreType.DMA((2, groups)),
        ],
        compiler_params=params(51),
    )(order, *hidden, weight)


def shift(array, axis, by):
    size = lax.axis_size(axis)
    return lax.ppermute(array, axis, [(i, (i + by) % size) for i in range(size)])


def from_earlier(array, axis, by):
    size = lax.axis_size(axis)
    return lax.ppermute(array, axis, [(i, i + by) for i in range(size - by)])


def spread(array, axis):
    copies = jnp.broadcast_to(array, (lax.axis_size(axis), *array.shape))
    return lax.all_to_all(copies, axis, 0, 0, tiled=True).reshape(-1, *array.shape[1:])


TURN = ((4, -3), (3, -2), (0, -1), (2, 1))


def to_columns(shard):
    pairs = []
    for z in range(16):
        for t in range(8):
            goal = z // 2
            far = TURN[(t // 2 - goal // 2) % 4][t % 2]
            pairs.append((z * 8 + t, (z + 2 * far) % 16 * 8 + goal))
    return lax.ppermute(shard, ("zh", "zl", "y", "c"), pairs)


def shards(queries, keys, values, norm_gain, out_weight):
    blocks = lax.axis_size("zl") * lax.axis_size("x")
    tp = lax.axis_size("y") * lax.axis_size("c")
    shard, state = lax.optimization_barrier((to_columns(out_weight.T), block_state(keys, values)))
    near = spread(shard, "x")
    pieces = lax.all_to_all(state, GROUP, 0, 0, tiled=True)
    weight = lax.all_gather(near, ("zh", "zl"), axis=0, tiled=True)
    weight = weight.reshape(tp, -1, out_weight.shape[0])

    total = group_total(pieces, blocks)
    earlier = []
    for group in range(lax.axis_size("zh") - 1):
        passed = total + earlier[-1] if earlier else total
        earlier.append(lax.ppermute(passed, "zh", [(group, group + 1)]))
    states = lax.all_to_all(prefix(pieces, earlier), GROUP, 0, 0, tiled=True)
    hidden = attend(queries, keys, values, states, norm_gain[None, :])

    steps = (0, 1, -1, 2)
    held = [hidden] + [shift(hidden, "y", by) for by in steps[1:]]
    held = held + [shift(h, "c", 1) for h in held]
    row, core = lax.axis_index("y"), lax.axis_index("c")
    far = jnp.array([TURN[-by % 4] for by in steps], jnp.int32)
    far = jnp.where(core == 0, far, far[:, ::-1]).T.reshape(-1)
    order = (row * 2 + core + far) % tp
    return project(order.astype(jnp.int32), held, weight)


def solution(mesh):
    axes = ("zh", "zl", "x", "y", "c")
    grid = Mesh(mesh.devices.reshape(4, 4, 4, 4, 2), axes)
    seq, tp = axes[:3], axes[3:]
    return jax.shard_map(
        shards,
        mesh=grid,
        in_specs=(P(seq, tp), P(seq, tp), P(seq, tp), P(tp), P(tp, seq)),
        out_specs=P(seq, tp),
        check_vma=False,
    )
```

```python
import functools

import jax
import jax.numpy as jnp
from jax import lax
from jax.experimental import pallas as pl
from jax.experimental.pallas import tpu as pltpu
from jax.sharding import Mesh, PartitionSpec as P

HEAD = 128
TILE = 256
PARTS = 2
NEAR = 5
GROUP = ("x", "zl")
NT = (((1,), (1,)), ((), ()))
TN = (((0,), (0,)), ((), ()))


def params(mib):
    return pltpu.CompilerParams(vmem_limit_bytes=mib * 1024 * 1024)


def in_vmem():
    return pl.BlockSpec(memory_space=pltpu.VMEM)


def in_hbm():
    return pl.BlockSpec(memory_space=pltpu.HBM)


def fetch(sources, buffers, sems):
    parts = sems.shape[1]
    copies = []
    for part in range(parts):
        for at, (source, buffer) in enumerate(zip(sources, buffers)):
            rows = source.shape[0] // parts
            own = pl.ds(part * rows, rows)
            copies.append(pltpu.make_async_copy(source.at[own], buffer.at[own], sems.at[at, part]))
    for copy in copies:
        copy.start()
    for copy in copies:
        copy.wait()


def block_state_kernel(k_hbm, v_hbm, s_ref, k_ref, v_ref, sems):
    fetch((k_hbm, v_hbm), (k_ref, v_ref), sems)
    for h in range(k_ref.shape[1] // HEAD):
        cols = slice(h * HEAD, (h + 1) * HEAD)
        s_ref[cols, :] = lax.dot_general(k_ref[:, cols], v_ref[:, cols], TN, preferred_element_type=jnp.float32)


def block_state(keys, values):
    return pl.pallas_call(
        block_state_kernel,
        out_shape=jax.ShapeDtypeStruct((keys.shape[1], HEAD), jnp.float32),
        in_specs=[in_hbm()] * 2,
        out_specs=in_vmem(),
        scratch_shapes=[pltpu.VMEM(keys.shape, keys.dtype)] * 2 + [pltpu.SemaphoreType.DMA((2, PARTS))],
        compiler_params=params(32),
    )(keys, values)


def total_kernel(s_ref, t_ref):
    rows = t_ref.shape[0]
    total = s_ref[:rows, :]
    for b in range(1, s_ref.shape[0] // rows):
        total = total + s_ref[b * rows:(b + 1) * rows, :]
    t_ref[...] = total


def group_total(pieces, blocks):
    return pl.pallas_call(
        total_kernel,
        out_shape=jax.ShapeDtypeStruct((pieces.shape[0] // blocks, HEAD), jnp.float32),
        in_specs=[in_vmem()],
        out_specs=in_vmem(),
        compiler_params=params(32),
    )(pieces)


def prefix_kernel(s_ref, *refs):
    *earlier_refs, p_ref = refs
    rows = earlier_refs[0].shape[0]
    total = earlier_refs[0][...]
    for ref in earlier_refs[1:]:
        total = total + ref[...]
    for b in range(s_ref.shape[0] // rows):
        place = b % 4 * 4 + b // 4
        at = slice(place * rows, (place + 1) * rows)
        p_ref[at, :] = total
        total = total + s_ref[at, :]


def prefix(pieces, earlier):
    return pl.pallas_call(
        prefix_kernel,
        out_shape=jax.ShapeDtypeStruct(pieces.shape, jnp.float32),
        in_specs=[in_vmem()] * (1 + len(earlier)),
        out_specs=in_vmem(),
        compiler_params=params(32),
    )(pieces, *earlier)


def attend_kernel(q_hbm, k_hbm, v_hbm, s_ref, g_ref, o_ref, q_ref, k_ref, v_ref, sems):
    fetch((q_hbm, k_hbm, v_hbm), (q_ref, k_ref, v_ref), sems)
    rows, width = o_ref.shape
    row = lax.broadcasted_iota(jnp.int32, (TILE, TILE), 0)
    col = lax.broadcasted_iota(jnp.int32, (TILE, TILE), 1)
    causal = row >= col
    for h in range(width // HEAD):
        cols = slice(h * HEAD, (h + 1) * HEAD)
        state = s_ref[cols, :]
        high = state.astype(jnp.bfloat16)
        low = (state - high.astype(jnp.float32)).astype(jnp.bfloat16)
        for first in range(0, rows, TILE):
            own = slice(first, first + TILE)
            query = q_ref[own, cols]
            scores = lax.dot_general(query, k_ref[:first + TILE, cols], NT, preferred_element_type=jnp.float32)
            left = [query, query, jnp.where(causal, scores[:, first:], 0.0).astype(jnp.bfloat16)]
            right = [high, low, v_ref[own, cols]]
            if first:
                left.append(scores[:, :first].astype(jnp.bfloat16))
                right.append(v_ref[:first, cols])
            left, right = jnp.concatenate(left, axis=1), jnp.concatenate(right, axis=0)
            attended = jnp.dot(left, right, preferred_element_type=jnp.float32)
            meansq = jnp.mean(attended * attended, axis=-1, keepdims=True)
            o_ref[own, cols] = (attended * lax.rsqrt(meansq + 1e-06) * g_ref[:, cols]).astype(jnp.bfloat16)


def attend(queries, keys, values, states, gain):
    return pl.pallas_call(
        attend_kernel,
        out_shape=jax.ShapeDtypeStruct(queries.shape, jnp.bfloat16),
        in_specs=[in_hbm()] * 3 + [in_vmem()] * 2,
        out_specs=in_vmem(),
        scratch_shapes=[pltpu.VMEM(queries.shape, queries.dtype)] * 3 + [pltpu.SemaphoreType.DMA((3, PARTS))],
        compiler_params=params(32),
    )(queries, keys, values, states, gain)


def project_kernel(order_ref, *refs):
    *hidden_refs, w_hbm, o_hbm, h_ref, w_ref, o_ref, sems, out_sems = refs
    groups = len(hidden_refs)
    columns = o_ref.shape[1] // 2
    copies = [pltpu.make_async_copy(w_hbm.at[order_ref[at]], w_ref.at[at], sems.at[at]) for at in range(groups)]
    for at in range(NEAR, groups):
        copies.append(pltpu.make_async_copy(hidden_refs[at], h_ref.at[at - NEAR], sems.at[groups + at - NEAR]))
    for copy in copies:
        copy.start()
    total = None
    for at in range(groups):
        copies[at].wait()
        if at >= NEAR:
            copies[groups + at - NEAR].wait()
        part = hidden_refs[at][...] if at < NEAR else h_ref[at - NEAR]
        if at < groups - 1:
            product = lax.dot_general(part, w_ref[at], NT, preferred_element_type=jnp.float32)
            total = product if total is None else total + product
            continue
        outs = []
        for half in range(2):
            own = slice(half * columns, (half + 1) * columns)
            product = lax.dot_general(part, w_ref[at, own], NT, preferred_element_type=jnp.float32)
            o_ref[:, own] = (total[:, own] + product).astype(o_ref.dtype)
            place = pl.ds(half * columns, columns)
            outs.append(pltpu.make_async_copy(o_ref.at[:, place], o_hbm.at[:, place], out_sems.at[half]))
            outs[-1].start()
        for copy in outs:
            copy.wait()


def project(order, hidden, weight):
    groups = weight.shape[0]
    rows = hidden[0].shape[0]
    return pl.pallas_call(
        project_kernel,
        out_shape=jax.ShapeDtypeStruct((rows, weight.shape[1]), jnp.bfloat16),
        in_specs=[pl.BlockSpec(memory_space=pltpu.SMEM)]
        + [in_vmem()] * NEAR
        + [pl.BlockSpec(memory_space=pl.ANY)] * (groups - NEAR)
        + [in_hbm()],
        out_specs=in_hbm(),
        scratch_shapes=[
            pltpu.VMEM((groups - NEAR, *hidden[0].shape), hidden[0].dtype),
            pltpu.VMEM(weight.shape, weight.dtype),
            pltpu.VMEM((rows, weight.shape[1]), jnp.bfloat16),
            pltpu.SemaphoreType.DMA((2 * groups - NEAR,)),
            pltpu.SemaphoreType.DMA((2,)),
        ],
        compiler_params=params(51),
    )(order, *hidden, weight)


def shift(array, axis, by):
    size = lax.axis_size(axis)
    return lax.ppermute(array, axis, [(i, (i + by) % size) for i in range(size)])


def from_earlier(array, axis, by):
    size = lax.axis_size(axis)
    return lax.ppermute(array, axis, [(i, i + by) for i in range(size - by)])


def spread(array, axis):
    copies = jnp.broadcast_to(array, (lax.axis_size(axis), *array.shape))
    return lax.all_to_all(copies, axis, 0, 0, tiled=True).reshape(-1, *array.shape[1:])


TURN = ((4, -3), (3, -2), (0, -1), (2, 1))


def to_columns(shard):
    pairs = []
    for z in range(16):
        for t in range(8):
            goal = z // 2
            far = TURN[(t // 2 - goal // 2) % 4][t % 2]
            pairs.append((z * 8 + t, (z + 2 * far) % 16 * 8 + goal))
    return lax.ppermute(shard, ("zh", "zl", "y", "c"), pairs)


def shards(queries, keys, values, norm_gain, out_weight):
    blocks = lax.axis_size("zl") * lax.axis_size("x")
    tp = lax.axis_size("y") * lax.axis_size("c")
    shard, state = lax.optimization_barrier((to_columns(out_weight.T), block_state(keys, values)))
    near, state = lax.optimization_barrier((spread(shard, "x"), state))
    pieces = lax.all_to_all(state, GROUP, 0, 0, tiled=True)
    weight = lax.all_gather(near, ("zh", "zl"), axis=0, tiled=True)
    weight = weight.reshape(tp, -1, out_weight.shape[0])

    total = group_total(pieces, blocks)
    earlier = []
    for group in range(lax.axis_size("zh") - 1):
        passed = total + earlier[-1] if earlier else total
        earlier.append(lax.ppermute(passed, "zh", [(group, group + 1)]))
    states = lax.all_to_all(prefix(pieces, earlier), GROUP, 0, 0, tiled=True)
    hidden = attend(queries, keys, values, states, norm_gain[None, :])

    steps = (0, 1, -1, 2)
    held = [hidden] + [shift(hidden, "y", by) for by in steps[1:]]
    held = held + [shift(h, "c", 1) for h in held]
    row, core = lax.axis_index("y"), lax.axis_index("c")
    far = jnp.array([TURN[-by % 4] for by in steps], jnp.int32)
    far = jnp.where(core == 0, far, far[:, ::-1]).T.reshape(-1)
    order = (row * 2 + core + far) % tp
    return project(order.astype(jnp.int32), held, weight)


def solution(mesh):
    axes = ("zh", "zl", "x", "y", "c")
    grid = Mesh(mesh.devices.reshape(4, 4, 4, 4, 2), axes)
    seq, tp = axes[:3], axes[3:]
    return jax.shard_map(
        shards,
        mesh=grid,
        in_specs=(P(seq, tp), P(seq, tp), P(seq, tp), P(tp), P(tp, seq)),
        out_specs=P(seq, tp),
        check_vma=False,
    )
```

```python
import functools

import jax
import jax.numpy as jnp
from jax import lax
from jax.experimental import pallas as pl
from jax.experimental.pallas import tpu as pltpu
from jax.sharding import Mesh, PartitionSpec as P

HEAD = 128
TILE = 256
PARTS = 2
NEAR = 5
GROUP = ("x", "zl")
NT = (((1,), (1,)), ((), ()))
TN = (((0,), (0,)), ((), ()))


def params(mib):
    return pltpu.CompilerParams(vmem_limit_bytes=mib * 1024 * 1024)


def in_vmem():
    return pl.BlockSpec(memory_space=pltpu.VMEM)


def in_hbm():
    return pl.BlockSpec(memory_space=pltpu.HBM)


def fetch(sources, buffers, sems):
    parts = sems.shape[1]
    copies = []
    for part in range(parts):
        for at, (source, buffer) in enumerate(zip(sources, buffers)):
            rows = source.shape[0] // parts
            own = pl.ds(part * rows, rows)
            copies.append(pltpu.make_async_copy(source.at[own], buffer.at[own], sems.at[at, part]))
    for copy in copies:
        copy.start()
    for copy in copies:
        copy.wait()


def block_state_kernel(k_hbm, v_hbm, s_ref, k_ref, v_ref, sems):
    fetch((k_hbm, v_hbm), (k_ref, v_ref), sems)
    for h in range(k_ref.shape[1] // HEAD):
        cols = slice(h * HEAD, (h + 1) * HEAD)
        s_ref[cols, :] = lax.dot_general(k_ref[:, cols], v_ref[:, cols], TN, preferred_element_type=jnp.float32)


def block_state(keys, values):
    return pl.pallas_call(
        block_state_kernel,
        out_shape=jax.ShapeDtypeStruct((keys.shape[1], HEAD), jnp.float32),
        in_specs=[in_hbm()] * 2,
        out_specs=in_vmem(),
        scratch_shapes=[pltpu.VMEM(keys.shape, keys.dtype)] * 2 + [pltpu.SemaphoreType.DMA((2, PARTS))],
        compiler_params=params(32),
    )(keys, values)


def total_kernel(s_ref, t_ref):
    rows = t_ref.shape[0]
    total = s_ref[:rows, :]
    for b in range(1, s_ref.shape[0] // rows):
        total = total + s_ref[b * rows:(b + 1) * rows, :]
    t_ref[...] = total


def group_total(pieces, blocks):
    return pl.pallas_call(
        total_kernel,
        out_shape=jax.ShapeDtypeStruct((pieces.shape[0] // blocks, HEAD), jnp.float32),
        in_specs=[in_vmem()],
        out_specs=in_vmem(),
        compiler_params=params(32),
    )(pieces)


def prefix_kernel(s_ref, *refs):
    *earlier_refs, p_ref = refs
    rows = earlier_refs[0].shape[0]
    total = earlier_refs[0][...]
    for ref in earlier_refs[1:]:
        total = total + ref[...]
    for b in range(s_ref.shape[0] // rows):
        place = b % 4 * 4 + b // 4
        at = slice(place * rows, (place + 1) * rows)
        p_ref[at, :] = total
        total = total + s_ref[at, :]


def prefix(pieces, earlier):
    return pl.pallas_call(
        prefix_kernel,
        out_shape=jax.ShapeDtypeStruct(pieces.shape, jnp.float32),
        in_specs=[in_vmem()] * (1 + len(earlier)),
        out_specs=in_vmem(),
        compiler_params=params(32),
    )(pieces, *earlier)


def attend_kernel(q_hbm, k_hbm, v_hbm, s_ref, g_ref, o_ref, q_ref, k_ref, v_ref, sems):
    fetch((q_hbm, k_hbm, v_hbm), (q_ref, k_ref, v_ref), sems)
    rows, width = o_ref.shape
    row = lax.broadcasted_iota(jnp.int32, (TILE, TILE), 0)
    col = lax.broadcasted_iota(jnp.int32, (TILE, TILE), 1)
    causal = row >= col
    for h in range(width // HEAD):
        cols = slice(h * HEAD, (h + 1) * HEAD)
        state = s_ref[cols, :]
        high = state.astype(jnp.bfloat16)
        low = (state - high.astype(jnp.float32)).astype(jnp.bfloat16)
        for first in range(0, rows, TILE):
            own = slice(first, first + TILE)
            query = q_ref[own, cols]
            scores = lax.dot_general(query, k_ref[:first + TILE, cols], NT, preferred_element_type=jnp.float32)
            left = [query, query, jnp.where(causal, scores[:, first:], 0.0).astype(jnp.bfloat16)]
            right = [high, low, v_ref[own, cols]]
            if first:
                left.append(scores[:, :first].astype(jnp.bfloat16))
                right.append(v_ref[:first, cols])
            left, right = jnp.concatenate(left, axis=1), jnp.concatenate(right, axis=0)
            attended = jnp.dot(left, right, preferred_element_type=jnp.float32)
            meansq = jnp.mean(attended * attended, axis=-1, keepdims=True)
            o_ref[own, cols] = (attended * lax.rsqrt(meansq + 1e-06) * g_ref[:, cols]).astype(jnp.bfloat16)


def attend(queries, keys, values, states, gain):
    return pl.pallas_call(
        attend_kernel,
        out_shape=jax.ShapeDtypeStruct(queries.shape, jnp.bfloat16),
        in_specs=[in_hbm()] * 3 + [in_vmem()] * 2,
        out_specs=in_vmem(),
        scratch_shapes=[pltpu.VMEM(queries.shape, queries.dtype)] * 3 + [pltpu.SemaphoreType.DMA((3, PARTS))],
        compiler_params=params(32),
    )(queries, keys, values, states, gain)


def project_kernel(order_ref, *refs):
    *hidden_refs, w_hbm, o_hbm, h_ref, w_ref, o_ref, sems, out_sems = refs
    groups = len(hidden_refs)
    copies = [pltpu.make_async_copy(w_hbm.at[order_ref[at]], w_ref.at[at], sems.at[at]) for at in range(groups)]
    for at in range(NEAR, groups):
        copies.append(pltpu.make_async_copy(hidden_refs[at], h_ref.at[at - NEAR], sems.at[groups + at - NEAR]))
    for copy in copies:
        copy.start()
    rows = o_ref.shape[0] // 2
    outs = []
    for half in range(2):
        own = slice(half * rows, (half + 1) * rows)
        total = None
        for at in range(groups):
            if half == 0:
                copies[at].wait()
                if at >= NEAR:
                    copies[groups + at - NEAR].wait()
            part = hidden_refs[at][own, :] if at < NEAR else h_ref[at - NEAR, own]
            product = lax.dot_general(part, w_ref[at], NT, preferred_element_type=jnp.float32)
            total = product if total is None else total + product
        o_ref[own, :] = total.astype(o_ref.dtype)
        place = pl.ds(half * rows, rows)
        outs.append(pltpu.make_async_copy(o_ref.at[place], o_hbm.at[place], out_sems.at[half]))
        outs[-1].start()
    for copy in outs:
        copy.wait()


def project(order, hidden, weight):
    groups = weight.shape[0]
    rows = hidden[0].shape[0]
    return pl.pallas_call(
        project_kernel,
        out_shape=jax.ShapeDtypeStruct((rows, weight.shape[1]), jnp.bfloat16),
        in_specs=[pl.BlockSpec(memory_space=pltpu.SMEM)]
        + [in_vmem()] * NEAR
        + [pl.BlockSpec(memory_space=pl.ANY)] * (groups - NEAR)
        + [in_hbm()],
        out_specs=in_hbm(),
        scratch_shapes=[
            pltpu.VMEM((groups - NEAR, *hidden[0].shape), hidden[0].dtype),
            pltpu.VMEM(weight.shape, weight.dtype),
            pltpu.VMEM((rows, weight.shape[1]), jnp.bfloat16),
            pltpu.SemaphoreType.DMA((2 * groups - NEAR,)),
            pltpu.SemaphoreType.DMA((2,)),
        ],
        compiler_params=params(51),
    )(order, *hidden, weight)


def shift(array, axis, by):
    size = lax.axis_size(axis)
    return lax.ppermute(array, axis, [(i, (i + by) % size) for i in range(size)])


def from_earlier(array, axis, by):
    size = lax.axis_size(axis)
    return lax.ppermute(array, axis, [(i, i + by) for i in range(size - by)])


def spread(array, axis):
    copies = jnp.broadcast_to(array, (lax.axis_size(axis), *array.shape))
    return lax.all_to_all(copies, axis, 0, 0, tiled=True).reshape(-1, *array.shape[1:])


TURN = ((4, -3), (3, -2), (0, -1), (2, 1))


def to_columns(shard):
    pairs = []
    for z in range(16):
        for t in range(8):
            goal = z // 2
            far = TURN[(t // 2 - goal // 2) % 4][t % 2]
            pairs.append((z * 8 + t, (z + 2 * far) % 16 * 8 + goal))
    return lax.ppermute(shard, ("zh", "zl", "y", "c"), pairs)


def shards(queries, keys, values, norm_gain, out_weight):
    blocks = lax.axis_size("zl") * lax.axis_size("x")
    tp = lax.axis_size("y") * lax.axis_size("c")
    shard, state = lax.optimization_barrier((to_columns(out_weight.T), block_state(keys, values)))
    near, state = lax.optimization_barrier((spread(shard, "x"), state))
    pieces = lax.all_to_all(state, GROUP, 0, 0, tiled=True)
    weight = lax.all_gather(near, ("zh", "zl"), axis=0, tiled=True)
    weight = weight.reshape(tp, -1, out_weight.shape[0])

    total = group_total(pieces, blocks)
    earlier = []
    for group in range(lax.axis_size("zh") - 1):
        passed = total + earlier[-1] if earlier else total
        earlier.append(lax.ppermute(passed, "zh", [(group, group + 1)]))
    states = lax.all_to_all(prefix(pieces, earlier), GROUP, 0, 0, tiled=True)
    hidden = attend(queries, keys, values, states, norm_gain[None, :])

    steps = (0, 1, -1, 2)
    held = [hidden] + [shift(hidden, "y", by) for by in steps[1:]]
    held = held + [shift(h, "c", 1) for h in held]
    row, core = lax.axis_index("y"), lax.axis_index("c")
    far = jnp.array([TURN[-by % 4] for by in steps], jnp.int32)
    far = jnp.where(core == 0, far, far[:, ::-1]).T.reshape(-1)
    order = (row * 2 + core + far) % tp
    return project(order.astype(jnp.int32), held, weight)


def solution(mesh):
    axes = ("zh", "zl", "x", "y", "c")
    grid = Mesh(mesh.devices.reshape(4, 4, 4, 4, 2), axes)
    seq, tp = axes[:3], axes[3:]
    return jax.shard_map(
        shards,
        mesh=grid,
        in_specs=(P(seq, tp), P(seq, tp), P(seq, tp), P(tp), P(tp, seq)),
        out_specs=P(seq, tp),
        check_vma=False,
    )
```
